32 devices in a mesh: groups: 1, gx: 32 (over z, y, x, core).
Axes of the slice: x: 2, y: 2, z: 4, core: 2. Of those that a mesh axis runs over, the one named last changes fastest.
Arguments:
- solid_state: float32 [9, 2, 1, 256, 4, 128], P(None, None, 'groups', 'gx'), may hold values from -6 to 6
- water_state: float32 [4, 2, 1, 128, 12, 256], P(None, None, 'groups', 'gx'), may hold values from -6 to 6
- lame_lambda: float32 [256, 4, 128], P('gx'), may hold values from 0.4 to 1.2
- shear_mu: float32 [256, 4, 128], P('gx'), may hold values from 0.1 to 0.5
- solid_buoy: float32 [256, 4, 128], P('gx'), may hold values from 0.4 to 1
- water_kappa: float32 [128, 12, 256], P('gx'), may hold values from 0.5 to 1
- water_buoy: float32 [128, 12, 256], P('gx'), may hold values from 0.6 to 1.2
- seafloor: int32 [128, 256], P('gx'), may hold values from 6 to 12
- source_cell: int32 [1], P('groups'), may hold values from 0 to 196607
- wavelet: float32 [4, 1], P(None, 'groups'), may hold values from -48 to 48
- receiver_column: int32 [128], replicated, may hold values from 0 to 32767
- observed: float32 [4, 1, 128], P(None, 'groups'), may hold values from -6 to 6
Outputs:
- grad_lambda: float32 [256, 4, 128], P('gx', 'groups')
- grad_mu: float32 [256, 4, 128], P('gx', 'groups')
- grad_kappa: float32 [128, 12, 256], P('gx', 'groups')
- residuals: float32 [4, 1, 128], P(None, 'groups')
The draws below stay inside these ranges and needn't reach their ends.
Inputs may be any that keep to these rules, and one draw needn't show every extreme that they name: Every column holds water from z = 0 to z = seafloor - 1 and rock below it. source_cell is (z * 128 + y) * 256 + x of a water cell with z below 6. receiver_column is y * 256 + x; two nodes may share a column.
All inputs are finite; a program needn't handle non-finite values.
Results may differ from the reference program's by a relative error of at most 0.00014.
Values sent between devices are 32-bit elements; how exact they have to be, the bound alone decides.
A program may use at most 64 MiB of HBM per device.

```python
import jax
import jax.numpy as jnp
from jax import lax

NZ = 4
WZ = 12
S = 1
R = 128
STEPS = 4
NX = 256
NY = 128


def plant(values, key, smallest, high):
    extent = values.shape
    place = [jax.random.randint(jax.random.fold_in(key, axis), (), 0, extent[axis]) for axis in range(len(extent))]
    values = values.at[tuple(place)].set(smallest)
    longest = extent.index(max(extent))
    place[longest] = (place[longest] + 1) % extent[longest]
    return values.at[tuple(place)].set(high)


def shard_levels(rng, shape, cuts, low, largest):
    def one(axis_at, blocks):
        heights = jax.random.uniform(jax.random.fold_in(jax.random.fold_in(rng, 6), axis_at), (blocks,), jnp.float32, low / len(cuts), largest / len(cuts))
        return jnp.repeat(jnp.exp(heights), shape[axis_at] // blocks).reshape((-1,) + (1,) * (len(shape) - axis_at - 1))

    level = one(*cuts[0])
    for cut in cuts[1:]:
        level = level * one(*cut)
    return level


def scatter_about(rng, extent, scale, most, split=(), held_as=jnp.bfloat16):
    factor_of = shard_levels(rng, extent, split, -0.22, 0.18) if split else 1.0
    entries = jax.random.normal(rng, extent, jnp.float32) * scale * factor_of
    return jnp.minimum(jnp.maximum(entries, -most), most).astype(held_as)


def setup_inputs(seed: int = 0, part: int = 0) -> dict:
    seeds = jax.random.split(jax.random.key(seed), 13)
    part_splits = jax.random.split(jax.random.fold_in(seeds[12], part), 13)
    return {
        "solid_state": scatter_about(part_splits[0], (9, 2, S, NX, NZ, NY), 1.0, 6.0, ((3, 32),), jnp.float32),
        "water_state": scatter_about(part_splits[1], (4, 2, S, NY, WZ, NX), 1.0, 6.0, ((3, 32),), jnp.float32),
        "lame_lambda": jnp.clip(0.4 + 0.800000042 * jax.random.uniform(seeds[2], (NX, NZ, NY), jnp.float32) ** shard_levels(seeds[2], (NX, NZ, NY), ((0, 32),), -0.2, 0.2), 0.4, 1.2),
        "shear_mu": jnp.clip(0.1 + 0.4 * jax.random.uniform(seeds[3], (NX, NZ, NY), jnp.float32) ** shard_levels(seeds[3], (NX, NZ, NY), ((0, 32),), -0.2, 0.2), 0.1, 0.5),
        "solid_buoy": jnp.clip(0.4 + 0.6 * jax.random.uniform(seeds[4], (NX, NZ, NY), jnp.float32) ** shard_levels(seeds[4], (NX, NZ, NY), ((0, 32),), -0.2, 0.2), 0.4, 1.0),
        "water_kappa": jnp.clip(0.5 + 0.5 * jax.random.uniform(seeds[5], (NY, WZ, NX), jnp.float32) ** shard_levels(seeds[5], (NY, WZ, NX), ((0, 32),), -0.2, 0.2), 0.5, 1.0),
        "water_buoy": jnp.clip(0.6 + 0.6 * jax.random.uniform(seeds[6], (NY, WZ, NX), jnp.float32) ** shard_levels(seeds[6], (NY, WZ, NX), ((0, 32),), -0.2, 0.2), 0.6, 1.2),
        "seafloor": plant(jax.random.randint(seeds[7], (NY, NX), WZ // 2, WZ + 1), jax.random.fold_in(seeds[7], 1), WZ // 2, WZ).astype(jnp.int32),
        "source_cell": jax.random.randint(part_splits[8], (S,), 0, (WZ // 2) * NY * NX).astype(jnp.int32),
        "wavelet": scatter_about(part_splits[9], (STEPS, S), 8.0, 48.0, (), jnp.float32),
        "receiver_column": plant(jax.random.randint(seeds[10], (R,), 0, NX * NY), jax.random.fold_in(seeds[10], 1), 0, (NX * NY) - 1).astype(jnp.int32),
        "observed": scatter_about(part_splits[11], (STEPS, S, R), 1.0, 6.0, (), jnp.float32),
    }


COEFF = (1225.0 / 1024.0, -245.0 / 3072.0, 49.0 / 5120.0, -5.0 / 7168.0)
TIME_STEP = 0.2

def stencil(padded, axis, forward):
    length = padded.shape[axis] - 8
    summed = None
    for offset in range(1, 5):
        if forward:
            front_at, back_at = (4 + offset, 5 - offset)
        else:
            front_at, back_at = (3 + offset, 4 - offset)
        front = lax.slice_in_dim(padded, front_at, front_at + length, axis=axis)
        back = lax.slice_in_dim(padded, back_at, back_at + length, axis=axis)
        addend = COEFF[offset - 1] * (front - back)
        summed = addend if summed is None else summed + addend
    return summed

def padded_zero(field, axis):
    widths = [(0, 0)] * field.ndim
    widths[axis] = (4, 4)
    return jnp.pad(field, widths)

def derive(field, axis, forward):
    return stencil(padded_zero(field, axis), axis, forward)

def reference(solid_state, water_state, lame_lambda, shear_mu, solid_buoy, water_kappa, water_buoy, seafloor, source_cell, wavelet, receiver_column, observed):
    vel_x, vel_y, vel_z = (solid_state[0], solid_state[1], solid_state[2])
    sig_xx, sig_yy, sig_zz = (solid_state[3], solid_state[4], solid_state[5])
    sig_xy, sig_xz, sig_yz = (solid_state[6], solid_state[7], solid_state[8])
    pressure, flow_x, flow_y, flow_z = (water_state[0], water_state[1], water_state[2], water_state[3])
    total_y, depth_rows, total_x = water_kappa.shape
    depth_idx = lax.broadcasted_iota(jnp.int32, (1, depth_rows, 1), 1)
    floor_rows = seafloor[:, None, :]
    live = (depth_idx < floor_rows).astype(jnp.float32)
    bottom = (depth_idx == floor_rows - 1).astype(jnp.float32)
    above = (depth_idx < floor_rows - 1).astype(jnp.float32)
    rows_y = lax.broadcasted_iota(jnp.int32, (total_y, 1, 1), 0)
    cols_x = lax.broadcasted_iota(jnp.int32, (1, 1, total_x), 2)
    flat_cell = (depth_idx * total_y + rows_y) * total_x + cols_x
    source_hot = (flat_cell[None] == source_cell[:, None, None, None]).astype(jnp.float32)
    node_y = receiver_column // total_x
    node_x = receiver_column % total_x
    grad_lambda = jnp.zeros(lame_lambda.shape, jnp.float32)
    grad_mu = jnp.zeros(lame_lambda.shape, jnp.float32)
    grad_kappa = jnp.zeros(water_kappa.shape, jnp.float32)
    misfits = []
    for step in range(wavelet.shape[0]):
        floor_pressure = lax.optimization_barrier(jnp.sum(pressure * bottom, axis=3))
        vel_x = vel_x + TIME_STEP * solid_buoy * (derive(sig_xx, 2, True) + derive(sig_xy, 4, False) + derive(sig_xz, 3, False))
        vel_y = vel_y + TIME_STEP * solid_buoy * (derive(sig_xy, 2, False) + derive(sig_yy, 4, True) + derive(sig_yz, 3, False))
        vel_z = vel_z + TIME_STEP * solid_buoy * (derive(sig_xz, 2, False) + derive(sig_yz, 4, False) + derive(sig_zz, 3, True))
        floor_velocity = jnp.transpose(vel_z[:, :, :, 0, :], (0, 1, 3, 2))
        flow_x = (flow_x - TIME_STEP * water_buoy * derive(pressure, 4, True)) * live
        flow_y = (flow_y - TIME_STEP * water_buoy * derive(pressure, 2, True)) * live
        flow_z = (flow_z - TIME_STEP * water_buoy * derive(pressure, 3, True)) * above + floor_velocity[:, :, :, None, :] * bottom
        strain_x = derive(vel_x, 2, False)
        strain_y = derive(vel_y, 4, False)
        strain_z = derive(vel_z, 3, False)
        dilation = strain_x + strain_y + strain_z
        shear_xy = derive(vel_x, 4, True) + derive(vel_y, 2, True)
        shear_xz = derive(vel_x, 3, True) + derive(vel_z, 2, True)
        shear_yz = derive(vel_y, 3, True) + derive(vel_z, 4, True)
        lam_part = lame_lambda * dilation
        sig_xx = sig_xx + TIME_STEP * (lam_part + 2.0 * shear_mu * strain_x)
        sig_yy = sig_yy + TIME_STEP * (lam_part + 2.0 * shear_mu * strain_y)
        sig_zz = sig_zz + TIME_STEP * (lam_part + 2.0 * shear_mu * strain_z)
        sig_xy = sig_xy + TIME_STEP * shear_mu * shear_xy
        sig_xz = sig_xz + TIME_STEP * shear_mu * shear_xz
        sig_yz = sig_yz + TIME_STEP * shear_mu * shear_yz
        sig_zz = sig_zz.at[:, :, :, 0, :].set(-jnp.transpose(floor_pressure, (0, 1, 3, 2)))
        grad_lambda = grad_lambda + lax.optimization_barrier(jnp.sum(dilation[0] * dilation[1], axis=0))
        normal_part = strain_x[0] * strain_x[1] + strain_y[0] * strain_y[1] + strain_z[0] * strain_z[1]
        shear_part = shear_xy[0] * shear_xy[1] + shear_xz[0] * shear_xz[1] + shear_yz[0] * shear_yz[1]
        grad_mu = grad_mu + lax.optimization_barrier(jnp.sum(2.0 * normal_part + shear_part, axis=0))
        pressure = (pressure - TIME_STEP * water_kappa * (derive(flow_x, 4, False) + derive(flow_y, 2, False) + derive(flow_z, 3, False))) * live
        pressure = pressure.at[0].add(wavelet[step][:, None, None, None] * source_hot)
        surface = lax.optimization_barrier(jnp.sum(pressure * bottom, axis=3))
        recorded = surface[0][:, node_y, node_x]
        misfit = recorded - observed[step]
        scaled = misfit * lax.rsqrt(lax.optimization_barrier(jnp.mean(misfit * misfit, axis=1, keepdims=True)) + 1e-06)
        inject = jnp.zeros(surface.shape[1:], jnp.float32).at[:, node_y, node_x].add(scaled)
        pressure = pressure.at[1].add(inject[:, :, None, :] * bottom)
        grad_kappa = grad_kappa + lax.optimization_barrier(jnp.sum(pressure[0] * pressure[1], axis=0))
        misfits.append(misfit)
    return (grad_lambda, grad_mu, grad_kappa, jnp.stack(misfits))
```

```python
import functools

import jax
import jax.numpy as jnp
from jax import lax
from jax.experimental import pallas as pl
from jax.experimental.pallas import tpu as pltpu
from jax.sharding import PartitionSpec as P

COEFF = (1225.0 / 1024.0, -245.0 / 3072.0, 49.0 / 5120.0, -5.0 / 7168.0)
DT = 0.2
EXACT = lax.Precision.HIGHEST
MESH = pl.DeviceIdType.MESH


def combine(at, forward):
    total = None
    for k in range(1, 5):
        term = at(k) - at(1 - k) if forward else at(k - 1) - at(-k)
        term = COEFF[k - 1] * term
        total = term if total is None else total + term
    return total


def along_z(f, forward):
    depth = f.shape[0]
    zeros = jnp.zeros((4,) + f.shape[1:], f.dtype)
    padded = jnp.concatenate([zeros, f, zeros], axis=0)
    return combine(lambda k: padded[4 + k : 4 + k + depth], forward)


def along_x(f, forward):
    size = f.shape[-1]
    lane = lax.broadcasted_iota(jnp.int32, f.shape, f.ndim - 1)

    def at(k):
        if k == 0:
            return f
        moved = pltpu.roll(f, (-k) % size, f.ndim - 1)
        keep = lane < size - k if k > 0 else lane >= -k
        return jnp.where(keep, moved, 0.0)

    return combine(at, forward)


def along_y(f, before, after, forward):
    axis = f.ndim - 2
    rows = f.shape[axis]
    tile = rows // 2
    row = lax.broadcasted_iota(jnp.int32, f.shape, axis) % tile

    def turn(a, s):
        s = s % rows
        return a if s == 0 else pltpu.roll(a, s, axis)

    def at(k):
        if k == 0:
            return f
        if k == tile:
            return after
        if k == -tile:
            return before
        if k > 0:
            return jnp.where(row < tile - k, turn(f, -k), turn(after, tile - k))
        return jnp.where(row >= -k, turn(f, -k), turn(before, -k - tile))

    return combine(at, forward)


def kernel(
    n, steps, total_y, total_x,
    rock, water, rock_par, water_par, floor, node_x, node_y, observed, source, wavelet,
    g_lambda, g_mu, g_kappa, residuals,
    state, flow, p_cur, inj,
    sig_buf, vel_buf, uy_buf, p_buf,
    sig_in, vel_in, uy_in, p_in, rec_buf, rec_in,
    sig_s, sig_r, vel_s, vel_r, uy_s, uy_r, p_s, p_r, rec_s, rec_r,
):
    me = lax.axis_index("gx")
    nz = rock.shape[1]
    wz, rows, width = water.shape[1:]
    tile = rows // 2

    def peer(s):
        return lax.rem(me + 1 + s, n)

    barrier = pltpu.get_barrier_semaphore()

    @pl.loop(0, n - 1)
    def _(s):
        pl.semaphore_signal(barrier, inc=1, device_id={"gx": peer(s)}, device_id_type=MESH)

    state[0] = rock[0]
    state[1] = rock[1]
    state[2] = rock[2]
    state[3] = rock[3]
    state[4] = rock[5]
    state[5] = rock[7]
    sig_buf[0, 0:nz] = rock[6]
    sig_buf[0, nz : 2 * nz] = rock[4]
    sig_buf[0, 2 * nz : 3 * nz] = rock[8]
    p_buf[0, 0:wz] = water[0]
    floor_f = floor[...].astype(jnp.float32)
    p_buf[0, wz] = floor_f
    p_cur[...] = water[0]
    flow[...] = water[1:4]
    inj[...] = jnp.zeros(inj.shape, jnp.float32)
    g_lambda[...] = jnp.zeros(g_lambda.shape, jnp.float32)
    g_mu[...] = jnp.zeros(g_mu.shape, jnp.float32)
    g_kappa[...] = jnp.zeros(g_kappa.shape, jnp.float32)

    for edge, slot in ((0, 0), (n - 1, 1)):

        @pl.when(me == edge)
        def _():
            for buf in (sig_in, vel_in, uy_in, p_in):
                buf[:, slot] = jnp.zeros(buf.shape[:1] + buf.shape[2:], jnp.float32)

    pl.semaphore_wait(barrier, n - 1)

    def copies(buf, into, send, recv, t):
        to_before = pltpu.make_async_remote_copy(
            src_ref=buf.at[t], dst_ref=into.at[t, 1], send_sem=send.at[t, 0], recv_sem=recv.at[t, 1],
            device_id={"gx": jnp.maximum(me - 1, 0)}, device_id_type=MESH)
        to_after = pltpu.make_async_remote_copy(
            src_ref=buf.at[t], dst_ref=into.at[t, 0], send_sem=send.at[t, 1], recv_sem=recv.at[t, 0],
            device_id={"gx": jnp.minimum(me + 1, n - 1)}, device_id_type=MESH)
        return to_before, to_after

    def start(*which):
        to_before, to_after = copies(*which)

        @pl.when(me > 0)
        def _():
            to_before.start()

        @pl.when(me < n - 1)
        def _():
            to_after.start()

    def arrive(*which):
        to_before, to_after = copies(*which)

        @pl.when(me > 0)
        def _():
            to_after.wait_recv()

        @pl.when(me < n - 1)
        def _():
            to_before.wait_recv()

    def sent(*which):
        to_before, to_after = copies(*which)

        @pl.when(me > 0)
        def _():
            to_before.wait_send()

        @pl.when(me < n - 1)
        def _():
            to_after.wait_send()

    sig = (sig_buf, sig_in, sig_s, sig_r)
    vel = (vel_buf, vel_in, vel_s, vel_r)
    uy = (uy_buf, uy_in, uy_s, uy_r)
    prs = (p_buf, p_in, p_s, p_r)

    start(*sig, 0)
    start(*prs, 0)

    z_idx = lax.broadcasted_iota(jnp.int32, (wz, rows, width), 0)
    row_idx = lax.broadcasted_iota(jnp.int32, (rows, 1), 0)
    y_in_tile = row_idx % tile
    floor_rows = floor[...][None]
    hot_x = (lax.broadcasted_iota(jnp.int32, (node_x.shape[0], width), 1) == node_x[...]).astype(jnp.float32)

    def bottom_of(rows_f):
        return (z_idx.astype(jnp.float32) == rows_f[None] - 1.0).astype(jnp.float32)

    def velocity(t):
        arrive(*sig, t)
        b = DT * rock_par[2]
        sxy, syy, syz = (sig_buf[t, i * nz : (i + 1) * nz] for i in range(3))
        lo = [sig_in[t, 0, i * nz : (i + 1) * nz] for i in range(3)]
        hi = [sig_in[t, 1, i * nz : (i + 1) * nz] for i in range(3)]
        sxx, szz, sxz = state[3], state[4], state[5]
        vx = state[0] + b * (along_x(sxx, True) + along_y(sxy, lo[0], hi[0], False) + along_z(sxz, False))
        vel_buf[t, 0:nz] = vx
        vy = state[1] + b * (along_x(sxy, False) + along_y(syy, lo[1], hi[1], True) + along_z(syz, False))
        vel_buf[t, nz : 2 * nz] = vy
        vz = state[2] + b * (along_x(sxz, False) + along_y(syz, lo[2], hi[2], False) + along_z(szz, True))
        vel_buf[t, 2 * nz : 3 * nz] = vz
        start(*vel, t)
        state[0] = vx
        state[1] = vy
        state[2] = vz

    velocity(0)

    def step(t, carry):
        live = (z_idx < floor_rows).astype(jnp.float32)
        bottom = (z_idx == floor_rows - 1).astype(jnp.float32)
        above = (z_idx < floor_rows - 1).astype(jnp.float32)
        p = p_cur[...]
        floor_p = jnp.sum(p * bottom, axis=0)
        b = DT * water_par[1]
        ux = (flow[0] - b * along_x(p, True)) * live
        flow[0] = ux
        floor_v = state[2, 0]
        uz = (flow[2] - b * along_z(p, True)) * above + floor_v[None] * bottom
        flow[2] = uz
        arrive(*prs, t)
        p_lo = p_in[t, 0, 0:wz] + inj[0][None] * bottom_of(p_in[t, 0, wz])
        p_hi = p_in[t, 1, 0:wz] + inj[1][None] * bottom_of(p_in[t, 1, wz])
        v = (flow[1] - b * along_y(p, p_lo, p_hi, True)) * live
        flow[1] = v
        uy_buf[t] = v
        start(*uy, t)

        arrive(*vel, t)
        vx, vy, vz = state[0], state[1], state[2]
        lo = [vel_in[t, 0, i * nz : (i + 1) * nz] for i in range(3)]
        hi = [vel_in[t, 1, i * nz : (i + 1) * nz] for i in range(3)]
        lam, mu = rock_par[0], rock_par[1]

        def pair(f):
            return f[:, 0:tile] * f[:, tile:rows]

        ex = along_x(vx, False)
        ey = along_y(vy, lo[1], hi[1], False)
        ez = along_z(vz, False)
        dilation = ex + ey + ez
        lam_part = lam * dilation
        state[3] = state[3] + DT * (lam_part + 2.0 * mu * ex)
        szz = state[4] + DT * (lam_part + 2.0 * mu * ez)
        state[4] = szz
        state[4, 0] = -floor_p
        sig_buf[t + 1, nz : 2 * nz] = sig_buf[t, nz : 2 * nz] + DT * (lam_part + 2.0 * mu * ey)
        gxy = along_y(vx, lo[0], hi[0], True) + along_x(vy, True)
        sig_buf[t + 1, 0:nz] = sig_buf[t, 0:nz] + DT * mu * gxy
        gyz = along_z(vy, True) + along_y(vz, lo[2], hi[2], True)
        sig_buf[t + 1, 2 * nz : 3 * nz] = sig_buf[t, 2 * nz : 3 * nz] + DT * mu * gyz

        @pl.when(t + 1 < steps)
        def _():
            start(*sig, t + 1)

        gxz = along_z(vx, True) + along_x(vz, True)
        state[5] = state[5] + DT * mu * gxz
        g_lambda[...] += pair(dilation)
        g_mu[...] += 2.0 * (pair(ex) + pair(ey) + pair(ez)) + (pair(gxy) + pair(gxz) + pair(gyz))

        partial = along_x(flow[0], False) + along_z(flow[2], False)
        arrive(*uy, t)
        p = (p_cur[...] - DT * water_par[0] * (
            partial + along_y(flow[1], uy_in[t, 0], uy_in[t, 1], False))) * live
        y_idx = me * tile + y_in_tile
        flat = (z_idx * total_y + y_idx[None]) * total_x + lax.broadcasted_iota(jnp.int32, z_idx.shape, 2)
        hit = (flat == source[0]) & (row_idx[None] < tile)
        p = p + jnp.where(hit, wavelet[t, 0], 0.0)
        p_buf[t + 1, 0:wz] = p
        p_buf[t + 1, wz] = floor_f

        @pl.when(t + 1 < steps)
        def _():
            start(*prs, t + 1)

        surface = jnp.sum(p * bottom, axis=0)
        picked = lax.dot_general(surface, hot_x, (((1,), (1,)), ((), ())), precision=EXACT,
                                 preferred_element_type=jnp.float32)
        mine = jnp.where((node_y[...] == y_idx) & (row_idx < tile), picked, 0.0)
        rec_buf[t] = mine

        @pl.loop(0, n - 1)
        def _(s):
            pltpu.make_async_remote_copy(
                src_ref=rec_buf.at[t], dst_ref=rec_in.at[t, s], send_sem=rec_s.at[t], recv_sem=rec_r.at[t],
                device_id={"gx": peer(s)}, device_id_type=MESH).start()

        @pl.when(t + 1 < steps)
        def _():
            velocity(t + 1)

        pltpu.make_async_copy(rec_in.at[t], rec_in.at[t], rec_r.at[t]).wait()
        every = jnp.sum(rec_in[t], axis=0) + mine
        misfit = jnp.sum(every, axis=0, keepdims=True) - observed[t]
        residuals[t] = misfit
        scaled = misfit * lax.rsqrt(jnp.mean(misfit * misfit, axis=1, keepdims=True) + 1e-06)

        def injected(shift):
            y_at = (me + shift) * tile + y_in_tile
            weight = jnp.where((node_y[...] == y_at) & (row_idx >= tile), scaled, 0.0)
            return jnp.dot(weight, hot_x, precision=EXACT, preferred_element_type=jnp.float32)

        inj[0] = injected(-1)
        inj[1] = injected(1)
        p = p_buf[t + 1, 0:wz] + injected(0)[None] * bottom
        p_cur[...] = p
        g_kappa[...] += pair(p)
        return carry

    lax.fori_loop(0, steps, step, 0)

    @pl.loop(0, steps)
    def _(t):
        sent(*sig, t)
        sent(*vel, t)
        sent(*uy, t)
        sent(*prs, t)
        pltpu.make_async_copy(rec_in.at[t], rec_in.at[t], rec_s.at[t]).wait()


def on_device(
    solid_state, water_state, lame_lambda, shear_mu, solid_buoy, water_kappa, water_buoy,
    seafloor, source_cell, wavelet, receiver_column, observed,
):
    n = lax.axis_size("gx")
    fields, waves, shots, wide, nz, total_y = solid_state.shape
    total_x = wide * n
    tile, wz = water_state.shape[3:5]
    steps, nodes = observed.shape[0], observed.shape[2]
    rows = waves * tile

    packed = jnp.concatenate(
        [solid_state.reshape(fields * waves, wide, nz, total_y), lame_lambda[None], shear_mu[None], solid_buoy[None]])
    count = packed.shape[0]
    packed = packed.reshape(count, wide, nz, n, tile).transpose(3, 0, 2, 4, 1)
    packed = lax.all_to_all(packed, "gx", 0, 0, tiled=True)
    packed = packed.transpose(1, 2, 3, 0, 4).reshape(count, nz, tile, total_x)
    rock = packed[: fields * waves].reshape(fields, waves, nz, tile, total_x)
    rock = rock.transpose(0, 2, 1, 3, 4).reshape(fields, nz, rows, total_x)
    rock_par = jnp.concatenate([packed[fields * waves :]] * 2, axis=2)
    water = water_state[:, :, 0].transpose(0, 3, 1, 2, 4).reshape(4, wz, rows, total_x)
    water_par = jnp.stack([water_kappa, water_buoy]).transpose(0, 2, 1, 3)
    water_par = jnp.concatenate([water_par] * 2, axis=2)
    floor = jnp.concatenate([seafloor] * 2, axis=0)
    node_x = (receiver_column % total_x)[:, None]
    node_y = (receiver_column // total_x)[None, :]

    f32 = jnp.float32
    plane = (rows, total_x)
    vmem = pl.BlockSpec(memory_space=pltpu.VMEM)
    smem = pl.BlockSpec(memory_space=pltpu.SMEM)
    pairs = pltpu.SemaphoreType.DMA((steps, 2))
    singles = pltpu.SemaphoreType.DMA((steps,))
    grad_lambda, grad_mu, grad_kappa, residuals = pl.pallas_call(
        functools.partial(kernel, n, steps, total_y, total_x),
        out_shape=(
            jax.ShapeDtypeStruct((nz, tile, total_x), f32),
            jax.ShapeDtypeStruct((nz, tile, total_x), f32),
            jax.ShapeDtypeStruct((wz, tile, total_x), f32),
            jax.ShapeDtypeStruct((steps, 1, nodes), f32),
        ),
        in_specs=[vmem] * 8 + [smem] * 2,
        out_specs=(vmem,) * 4,
        scratch_shapes=[
            pltpu.VMEM((6, nz) + plane, f32),
            pltpu.VMEM((3, wz) + plane, f32),
            pltpu.VMEM((wz,) + plane, f32),
            pltpu.VMEM((2,) + plane, f32),
            pltpu.VMEM((steps + 1, 3 * nz) + plane, f32),
            pltpu.VMEM((steps, 3 * nz) + plane, f32),
            pltpu.VMEM((steps, wz) + plane, f32),
            pltpu.VMEM((steps + 1, wz + 1) + plane, f32),
            pltpu.VMEM((steps, 2, 3 * nz) + plane, f32),
            pltpu.VMEM((steps, 2, 3 * nz) + plane, f32),
            pltpu.VMEM((steps, 2, wz) + plane, f32),
            pltpu.VMEM((steps, 2, wz + 1) + plane, f32),
            pltpu.VMEM((steps, rows, nodes), f32),
            pltpu.VMEM((steps, n - 1, rows, nodes), f32),
            pairs, pairs, pairs, pairs, pairs, pairs, pairs, pairs, singles, singles,
        ],
        compiler_params=pltpu.CompilerParams(
            collective_id=0, has_side_effects=True, vmem_limit_bytes=56 * 1024 * 1024),
    )(rock, water, rock_par, water_par, floor, node_x, node_y, observed, source_cell, wavelet)

    grads = jnp.stack([grad_lambda, grad_mu]).reshape(2, nz, tile, n, wide).transpose(3, 0, 1, 2, 4)
    grads = lax.all_to_all(grads, "gx", 0, 0, tiled=True)
    grads = grads.transpose(1, 4, 2, 0, 3).reshape(2, wide, nz, total_y)
    return grads[0], grads[1], grad_kappa.transpose(1, 0, 2), residuals


def solution(mesh):
    placed = (
        P(None, None, "groups", "gx", None, None),
        P(None, None, "groups", "gx", None, None),
        P("gx", None, None),
        P("gx", None, None),
        P("gx", None, None),
        P("gx", None, None),
        P("gx", None, None),
        P("gx", None),
        P("groups"),
        P(None, "groups"),
        P(),
        P(None, "groups", None),
    )
    return jax.shard_map(
        on_device,
        mesh=mesh,
        in_specs=placed,
        out_specs=(
            P("gx", "groups", None),
            P("gx", "groups", None),
            P("gx", "groups", None),
            P(None, "groups", None),
        ),
        check_vma=False,
    )
```

```python
import functools

import jax
import jax.numpy as jnp
from jax import lax
from jax.experimental import pallas as pl
from jax.experimental.pallas import tpu as pltpu
from jax.sharding import PartitionSpec as P

COEFF = (1225.0 / 1024.0, -245.0 / 3072.0, 49.0 / 5120.0, -5.0 / 7168.0)
DT = 0.2
MESH = pl.DeviceIdType.MESH


def combine(at, forward):
    total = None
    for k in range(1, 5):
        term = at(k) - at(1 - k) if forward else at(k - 1) - at(-k)
        term = COEFF[k - 1] * term
        total = term if total is None else total + term
    return total


def along_z(f, forward):
    depth = f.shape[0]
    zeros = jnp.zeros((4,) + f.shape[1:], f.dtype)
    padded = jnp.concatenate([zeros, f, zeros], axis=0)
    return combine(lambda k: padded[4 + k : 4 + k + depth], forward)


def along_x(f, forward):
    size = f.shape[-1]
    lane = lax.broadcasted_iota(jnp.int32, f.shape, f.ndim - 1)

    def at(k):
        if k == 0:
            return f
        moved = pltpu.roll(f, (-k) % size, f.ndim - 1)
        keep = lane < size - k if k > 0 else lane >= -k
        return jnp.where(keep, moved, 0.0)

    return combine(at, forward)


def along_y(f, before, after, forward):
    axis = f.ndim - 2
    rows = f.shape[axis]
    tile = rows // 2
    row = lax.broadcasted_iota(jnp.int32, f.shape, axis) % tile

    def turn(a, s):
        s = s % rows
        return a if s == 0 else pltpu.roll(a, s, axis)

    def at(k):
        if k == 0:
            return f
        if k == tile:
            return after
        if k == -tile:
            return before
        if k > 0:
            return jnp.where(row < tile - k, turn(f, -k), turn(after, tile - k))
        return jnp.where(row >= -k, turn(f, -k), turn(before, -k - tile))

    return combine(at, forward)


def exact_dot(a, hot, dims):
    high = a.astype(jnp.bfloat16).astype(jnp.float32)
    rest = a - high
    middle = rest.astype(jnp.bfloat16).astype(jnp.float32)
    split = jnp.concatenate([high, middle, rest - middle], axis=0).astype(jnp.bfloat16)
    out = lax.dot_general(split, hot, (dims, ((), ())), preferred_element_type=jnp.float32)
    m = a.shape[0]
    return out[0:m] + (out[m : 2 * m] + out[2 * m :])


def kernel(
    n, steps, total_y, total_x,
    solid, water, lame, mu_ref, buoy, kappa, wbuoy, floor_ref, nodes, observed, source, wavelet,
    out_lambda, out_mu, out_kappa, residuals,
    state, rock_par, flow, water_par, p_cur, inj,
    g_lambda, g_mu, g_kappa,
    rows_x, pack_out, pack_in, pack_all, grad_out, grad_in, grad_rows,
    sig_buf, vel_buf, uy_buf, p_buf,
    sig_in, vel_in, uy_in, p_in, rec_buf, rec_in,
    sig_s, sig_r, vel_s, vel_r, uy_s, uy_r, p_s, p_r, rec_s, rec_r, all_s, all_r,
):
    me = lax.axis_index("gx")
    wide, nz = lame.shape[0:2]
    wz, width = kappa.shape[1:]
    tile = kappa.shape[0]
    rows = 2 * tile
    f32 = jnp.float32

    def peer(s):
        return lax.rem(me + 1 + s, n)

    barrier = pltpu.get_barrier_semaphore()

    @pl.loop(0, n - 1)
    def _(s):
        pl.semaphore_signal(barrier, inc=1, device_id={"gx": peer(s)}, device_id_type=MESH)

    rows_x[...] = jnp.zeros(rows_x.shape, f32)
    for wave in range(2):
        for field in range(9):
            at = wave * 10 * nz + field * nz
            rows_x[:, at : at + nz, :] = solid[field, wave, 0]
    for i, ref in enumerate((lame, mu_ref, buoy)):
        at = (20 + i) * nz
        rows_x[:, at : at + nz, :] = ref[...]
    lane = lax.broadcasted_iota(jnp.int32, (total_y, 128), 1)
    y_of = lax.broadcasted_iota(jnp.int32, (total_y, 128), 0) % tile
    for x in range(wide):
        t0 = jnp.transpose(rows_x[x])
        t1, t2 = (pltpu.roll(t0, total_y - k, 0) for k in (1, 2))
        half = jnp.where(lane < 64, t0, pltpu.roll(t1, 64, 1))
        tb = pltpu.roll(t0, 1, 0)
        quarter = jnp.where(
            lane < 32, pltpu.roll(tb, 64, 1),
            jnp.where(lane < 64, pltpu.roll(t0, 96, 1), jnp.where(lane < 96, t1, pltpu.roll(t2, 32, 1))))
        pack_out[:, x, :] = jnp.where(y_of == 1, quarter, half)

    for wave in range(2):
        for y in range(tile):
            at = wave * tile + y
            p_buf[0, 0:wz, at, :] = water[0, wave, 0, y]
    floor = jnp.concatenate([floor_ref[...], floor_ref[...]], axis=0)
    floor_f = floor.astype(f32)
    p_buf[0, wz] = floor_f

    for edge, slot in ((0, 0), (n - 1, 1)):

        @pl.when(me == edge)
        def _():
            for buf in (sig_in, vel_in, uy_in, p_in):
                buf[:, slot] = jnp.zeros(buf.shape[:1] + buf.shape[2:], f32)

    pl.semaphore_wait(barrier, n - 1)

    @pl.loop(0, n - 1)
    def _(s):
        pltpu.make_async_remote_copy(
            src_ref=pack_out.at[pl.ds(peer(s) * tile, 3)], dst_ref=pack_in.at[s],
            send_sem=all_s.at[0], recv_sem=all_r.at[0],
            device_id={"gx": peer(s)}, device_id_type=MESH).start()

    pack_in[n - 1] = pack_out[pl.ds(me * tile, 3)]

    def copies(buf, into, send, recv, t):
        to_before = pltpu.make_async_remote_copy(
            src_ref=buf.at[t], dst_ref=into.at[t, 1], send_sem=send.at[t, 0], recv_sem=recv.at[t, 1],
            device_id={"gx": jnp.maximum(me - 1, 0)}, device_id_type=MESH)
        to_after = pltpu.make_async_remote_copy(
            src_ref=buf.at[t], dst_ref=into.at[t, 0], send_sem=send.at[t, 1], recv_sem=recv.at[t, 0],
            device_id={"gx": jnp.minimum(me + 1, n - 1)}, device_id_type=MESH)
        return to_before, to_after

    def start(*which):
        to_before, to_after = copies(*which)

        @pl.when(me > 0)
        def _():
            to_before.start()

        @pl.when(me < n - 1)
        def _():
            to_after.start()

    def arrive(*which):
        to_before, to_after = copies(*which)

        @pl.when(me > 0)
        def _():
            to_after.wait_recv()

        @pl.when(me < n - 1)
        def _():
            to_before.wait_recv()

    def sent(*which):
        to_before, to_after = copies(*which)

        @pl.when(me > 0)
        def _():
            to_before.wait_send()

        @pl.when(me < n - 1)
        def _():
            to_after.wait_send()

    sig = (sig_buf, sig_in, sig_s, sig_r)
    vel = (vel_buf, vel_in, vel_s, vel_r)
    uy = (uy_buf, uy_in, uy_s, uy_r)
    prs = (p_buf, p_in, p_s, p_r)

    start(*prs, 0)

    for wave in range(2):
        for y in range(tile):
            at = wave * tile + y
            for i in range(3):
                flow[i, :, at, :] = water[i + 1, wave, 0, y]
            water_par[0, :, at, :] = kappa[y]
            water_par[1, :, at, :] = wbuoy[y]
    p_cur[...] = p_buf[0, 0:wz]
    inj[...] = jnp.zeros(inj.shape, f32)
    g_lambda[...] = jnp.zeros(g_lambda.shape, f32)
    g_mu[...] = jnp.zeros(g_mu.shape, f32)
    g_kappa[...] = jnp.zeros(g_kappa.shape, f32)

    first = pl.ds(0, n - 1)
    pltpu.make_async_copy(pack_in.at[first], pack_in.at[first], all_r.at[0]).wait()

    @pl.loop(0, n)
    def _(src):
        pack_all[:, src] = pack_in[lax.rem(me - 1 - src + 2 * n, n)]

    whole = [jnp.transpose(pack_all[i].reshape(total_x, 128)) for i in range(3)]
    for y in range(tile):
        large = whole[0 if y < 2 else 2][(y % 2) * 64 : (y % 2) * 64 + 64]
        every = jnp.concatenate([large, whole[1][y * 32 : y * 32 + 32]], axis=0)
        for wave in range(2):
            at = wave * 10 * nz
            part = every[at : at + 9 * nz]
            for to, field in ((0, 0), (1, 1), (2, 2), (3, 3), (4, 5), (5, 7)):
                state[to, :, wave * tile + y, :] = part[field * nz : (field + 1) * nz]
            for to, field in enumerate((6, 4, 8)):
                sig_buf[0, to * nz : (to + 1) * nz, wave * tile + y, :] = part[field * nz : (field + 1) * nz]
            for i in range(3):
                rock_par[i, :, wave * tile + y, :] = every[(20 + i) * nz : (21 + i) * nz]

    start(*sig, 0)

    z_idx = lax.broadcasted_iota(jnp.int32, (wz, rows, width), 0)
    row_idx = lax.broadcasted_iota(jnp.int32, (rows, 1), 0)
    y_in_tile = row_idx % tile
    floor_rows = floor[None]
    node_x = nodes[...] % total_x
    node_y = nodes[...] // total_x
    hot_x = (lax.broadcasted_iota(jnp.int32, (width, nodes.shape[1]), 0) == node_x).astype(jnp.bfloat16)

    def bottom_of(rows_f):
        return (z_idx.astype(jnp.float32) == rows_f[None] - 1.0).astype(jnp.float32)

    def velocity(t):
        arrive(*sig, t)
        b = DT * rock_par[2]
        sxy, syy, syz = (sig_buf[t, i * nz : (i + 1) * nz] for i in range(3))
        lo = [sig_in[t, 0, i * nz : (i + 1) * nz] for i in range(3)]
        hi = [sig_in[t, 1, i * nz : (i + 1) * nz] for i in range(3)]
        sxx, szz, sxz = state[3], state[4], state[5]
        vx = state[0] + b * (along_x(sxx, True) + along_y(sxy, lo[0], hi[0], False) + along_z(sxz, False))
        vel_buf[t, 0:nz] = vx
        vy = state[1] + b * (along_x(sxy, False) + along_y(syy, lo[1], hi[1], True) + along_z(syz, False))
        vel_buf[t, nz : 2 * nz] = vy
        vz = state[2] + b * (along_x(sxz, False) + along_y(syz, lo[2], hi[2], False) + along_z(szz, True))
        vel_buf[t, 2 * nz : 3 * nz] = vz
        start(*vel, t)
        state[0] = vx
        state[1] = vy
        state[2] = vz

    velocity(0)

    def step(t, carry):
        live = (z_idx < floor_rows).astype(jnp.float32)
        bottom = (z_idx == floor_rows - 1).astype(jnp.float32)
        above = (z_idx < floor_rows - 1).astype(jnp.float32)
        p = p_cur[...]
        floor_p = jnp.sum(p * bottom, axis=0)
        b = DT * water_par[1]
        ux = (flow[0] - b * along_x(p, True)) * live
        flow[0] = ux
        floor_v = state[2, 0]
        uz = (flow[2] - b * along_z(p, True)) * above + floor_v[None] * bottom
        flow[2] = uz
        arrive(*prs, t)
        p_lo = p_in[t, 0, 0:wz] + inj[0][None] * bottom_of(p_in[t, 0, wz])
        p_hi = p_in[t, 1, 0:wz] + inj[1][None] * bottom_of(p_in[t, 1, wz])
        v = (flow[1] - b * along_y(p, p_lo, p_hi, True)) * live
        flow[1] = v
        uy_buf[t] = v
        start(*uy, t)

        arrive(*vel, t)
        vx, vy, vz = state[0], state[1], state[2]
        lo = [vel_in[t, 0, i * nz : (i + 1) * nz] for i in range(3)]
        hi = [vel_in[t, 1, i * nz : (i + 1) * nz] for i in range(3)]
        lam, mu = rock_par[0], rock_par[1]

        def pair(f):
            return f[:, 0:tile] * f[:, tile:rows]

        ex = along_x(vx, False)
        ey = along_y(vy, lo[1], hi[1], False)
        ez = along_z(vz, False)
        dilation = ex + ey + ez
        lam_part = lam * dilation
        state[3] = state[3] + DT * (lam_part + 2.0 * mu * ex)
        szz = state[4] + DT * (lam_part + 2.0 * mu * ez)
        state[4] = szz
        state[4, 0] = -floor_p
        sig_buf[t + 1, nz : 2 * nz] = sig_buf[t, nz : 2 * nz] + DT * (lam_part + 2.0 * mu * ey)
        gxy = along_y(vx, lo[0], hi[0], True) + along_x(vy, True)
        sig_buf[t + 1, 0:nz] = sig_buf[t, 0:nz] + DT * mu * gxy
        gyz = along_z(vy, True) + along_y(vz, lo[2], hi[2], True)
        sig_buf[t + 1, 2 * nz : 3 * nz] = sig_buf[t, 2 * nz : 3 * nz] + DT * mu * gyz

        @pl.when(t + 1 < steps)
        def _():
            start(*sig, t + 1)

        gxz = along_z(vx, True) + along_x(vz, True)
        state[5] = state[5] + DT * mu * gxz
        g_lambda[...] += pair(dilation)
        g_mu[...] += 2.0 * (pair(ex) + pair(ey) + pair(ez)) + (pair(gxy) + pair(gxz) + pair(gyz))

        partial = along_x(flow[0], False) + along_z(flow[2], False)
        arrive(*uy, t)
        p = (p_cur[...] - DT * water_par[0] * (
            partial + along_y(flow[1], uy_in[t, 0], uy_in[t, 1], False))) * live
        y_idx = me * tile + y_in_tile
        flat = (z_idx * total_y + y_idx[None]) * total_x + lax.broadcasted_iota(jnp.int32, z_idx.shape, 2)
        hit = (flat == source[0]) & (row_idx[None] < tile)
        p = p + jnp.where(hit, wavelet[pl.ds(t, 1)][None], 0.0)
        p_buf[t + 1, 0:wz] = p
        p_buf[t + 1, wz] = floor_f

        @pl.when(t + 1 < steps)
        def _():
            start(*prs, t + 1)

        surface = jnp.sum(p * bottom, axis=0)
        picked = exact_dot(surface, hot_x, ((1,), (0,)))
        mine = jnp.where((node_y == y_idx) & (row_idx < tile), picked, 0.0)
        rec_buf[t] = mine

        @pl.loop(0, n - 1)
        def _(s):
            pltpu.make_async_remote_copy(
                src_ref=rec_buf.at[t], dst_ref=rec_in.at[t, s], send_sem=rec_s.at[t], recv_sem=rec_r.at[t],
                device_id={"gx": peer(s)}, device_id_type=MESH).start()

        @pl.when(t + 1 < steps)
        def _():
            velocity(t + 1)

        pltpu.make_async_copy(rec_in.at[t], rec_in.at[t], rec_r.at[t]).wait()
        every = jnp.sum(rec_in[t], axis=0) + mine
        misfit = jnp.sum(every, axis=0, keepdims=True) - observed[t]
        residuals[t] = misfit
        scaled = misfit * lax.rsqrt(jnp.mean(misfit * misfit, axis=1, keepdims=True) + 1e-06)

        def weight(shift):
            y_at = (me + shift) * tile + y_in_tile
            return jnp.where((node_y == y_at) & (row_idx >= tile), scaled, 0.0)

        weights = jnp.concatenate([weight(-1), weight(1), weight(0)], axis=0)
        injected = exact_dot(weights, hot_x, ((1,), (1,)))
        inj[0] = injected[0:rows]
        inj[1] = injected[rows : 2 * rows]
        p = p_buf[t + 1, 0:wz] + injected[2 * rows :][None] * bottom
        p_cur[...] = p
        g_kappa[...] += pair(p)
        return carry

    lax.fori_loop(0, steps, step, 0)

    grad_rows[...] = jnp.zeros(grad_rows.shape, f32)
    for y in range(tile):
        grad_rows[y * 2 * nz : y * 2 * nz + nz] = g_lambda[:, y, :]
        grad_rows[y * 2 * nz + nz : (y + 1) * 2 * nz] = g_mu[:, y, :]
    grad_out[...] = jnp.transpose(grad_rows[...]).reshape(n, wide, 128)

    @pl.loop(0, n - 1)
    def _(s):
        pltpu.make_async_remote_copy(
            src_ref=grad_out.at[peer(s)], dst_ref=grad_in.at[s],
            send_sem=all_s.at[1], recv_sem=all_r.at[1],
            device_id={"gx": peer(s)}, device_id_type=MESH).start()

    grad_in[n - 1] = grad_out[me]
    for y in range(tile):
        out_kappa[y] = g_kappa[:, y, :]

    @pl.loop(0, steps)
    def _(t):
        sent(*sig, t)
        sent(*vel, t)
        sent(*uy, t)
        sent(*prs, t)
        pltpu.make_async_copy(rec_in.at[t], rec_in.at[t], rec_s.at[t]).wait()

    pltpu.make_async_copy(pack_in.at[first], pack_in.at[first], all_s.at[0]).wait()
    pltpu.make_async_copy(grad_in.at[first], grad_in.at[first], all_r.at[1]).wait()
    by_x = [[] for _ in range(tile)]
    column = lax.broadcasted_iota(jnp.int32, (n, total_y), 1)
    slot = lax.broadcasted_iota(jnp.int32, (n, total_y), 0)
    src = lax.rem(me - 1 - slot + 2 * n, n)
    for x in range(wide):
        turned = jnp.transpose(grad_in[:, x, :])
        for y in range(tile):
            by_x[y].append(turned[y * 2 * nz : (y + 1) * 2 * nz])
    total = None
    for y in range(tile):
        place = (column == src * tile + y).astype(jnp.bfloat16)
        part = exact_dot(jnp.concatenate(by_x[y], axis=0), place, ((1,), (0,)))
        total = part if total is None else total + part
    for x in range(wide):
        out_lambda[x] = total[x * 2 * nz : x * 2 * nz + nz]
        out_mu[x] = total[x * 2 * nz + nz : (x + 1) * 2 * nz]
    pltpu.make_async_copy(grad_in.at[first], grad_in.at[first], all_s.at[1]).wait()


def on_device(
    solid_state, water_state, lame_lambda, shear_mu, solid_buoy, water_kappa, water_buoy,
    seafloor, source_cell, wavelet, receiver_column, observed,
):
    n = lax.axis_size("gx")
    fields, waves, shots, wide, nz, total_y = solid_state.shape
    total_x = wide * n
    tile, wz = water_state.shape[3:5]
    steps, nodes = observed.shape[0], observed.shape[2]
    rows = waves * tile

    f32 = jnp.float32
    plane = (rows, total_x)
    vmem = pl.BlockSpec(memory_space=pltpu.VMEM)
    smem = pl.BlockSpec(memory_space=pltpu.SMEM)
    pairs = pltpu.SemaphoreType.DMA((steps, 2))
    ends = pltpu.SemaphoreType.DMA((2,))
    singles = pltpu.SemaphoreType.DMA((steps,))
    return pl.pallas_call(
        functools.partial(kernel, n, steps, total_y, total_x),
        out_shape=(
            jax.ShapeDtypeStruct((wide, nz, total_y), f32),
            jax.ShapeDtypeStruct((wide, nz, total_y), f32),
            jax.ShapeDtypeStruct((tile, wz, total_x), f32),
            jax.ShapeDtypeStruct((steps, 1, nodes), f32),
        ),
        in_specs=[vmem] * 10 + [smem, vmem],
        out_specs=(vmem,) * 4,
        scratch_shapes=[
            pltpu.VMEM((6, nz) + plane, f32),
            pltpu.VMEM((3, nz) + plane, f32),
            pltpu.VMEM((3, wz) + plane, f32),
            pltpu.VMEM((2, wz) + plane, f32),
            pltpu.VMEM((wz,) + plane, f32),
            pltpu.VMEM((2,) + plane, f32),
            pltpu.VMEM((nz, tile, total_x), f32),
            pltpu.VMEM((nz, tile, total_x), f32),
            pltpu.VMEM((wz, tile, total_x), f32),
            pltpu.VMEM((wide, 128, total_y), f32),
            pltpu.VMEM((total_y, wide, 128), f32),
            pltpu.VMEM((n, 3, wide, 128), f32),
            pltpu.VMEM((3, n, wide, 128), f32),
            pltpu.VMEM((n, wide, 128), f32),
            pltpu.VMEM((n, wide, 128), f32),
            pltpu.VMEM((128, total_x), f32),
            pltpu.VMEM((steps + 1, 3 * nz) + plane, f32),
            pltpu.VMEM((steps, 3 * nz) + plane, f32),
            pltpu.VMEM((steps, wz) + plane, f32),
            pltpu.VMEM((steps + 1, wz + 1) + plane, f32),
            pltpu.VMEM((steps, 2, 3 * nz) + plane, f32),
            pltpu.VMEM((steps, 2, 3 * nz) + plane, f32),
            pltpu.VMEM((steps, 2, wz) + plane, f32),
            pltpu.VMEM((steps, 2, wz + 1) + plane, f32),
            pltpu.VMEM((steps, rows, nodes), f32),
            pltpu.VMEM((steps, n - 1, rows, nodes), f32),
            pairs, pairs, pairs, pairs, pairs, pairs, pairs, pairs, singles, singles, ends, ends,
        ],
        compiler_params=pltpu.CompilerParams(
            collective_id=0, has_side_effects=True, vmem_limit_bytes=56 * 1024 * 1024),
    )(solid_state, water_state, lame_lambda, shear_mu, solid_buoy, water_kappa, water_buoy,
      seafloor, receiver_column[None, :], observed, source_cell, wavelet)


def solution(mesh):
    placed = (
        P(None, None, "groups", "gx", None, None),
        P(None, None, "groups", "gx", None, None),
        P("gx", None, None),
        P("gx", None, None),
        P("gx", None, None),
        P("gx", None, None),
        P("gx", None, None),
        P("gx", None),
        P("groups"),
        P(None, "groups"),
        P(),
        P(None, "groups", None),
    )
    return jax.shard_map(
        on_device,
        mesh=mesh,
        in_specs=placed,
        out_specs=(
            P("gx", "groups", None),
            P("gx", "groups", None),
            P("gx", "groups", None),
            P(None, "groups", None),
        ),
        check_vma=False,
    )
```
